512 devices in a mesh: segment: 4 (over z_lo), expert: 128 (over z_hi, y, x, core).
Axes of the slice: x: 4, y: 8, z: 8 (z_hi: 2, z_lo: 4; z = z_hi * 4 + z_lo), core: 2. Of those that a mesh axis runs over, the one named last changes fastest.
Arguments:
- forward_input: bfloat16 [4, 1024, 2048], P('segment', 'expert'), may hold values from -6 to 6
- forward_routes: int32 [4, 1024, 6], P('segment', 'expert'), may hold values from 0 to 31, all different within a row; in each aligned block of 8 rows (0 to 7, 8 to 15, ..., all dimensions but the last counted through in order) at most 2 rows name the same one
- forward_gates: float32 [4, 1024, 6], P('segment', 'expert'), may hold values from 0.1 to 1
- backward_grad: bfloat16 [4, 1024, 2048], P('segment', 'expert'), may hold values from -6 to 6
- backward_routes: int32 [4, 1024, 6], P('segment', 'expert'), may hold values from 0 to 31, all different within a row; in each aligned block of 8 rows (0 to 7, 8 to 15, ..., all dimensions but the last counted through in order) at most 2 rows name the same one
- backward_gates: float32 [4, 1024, 6], P('segment', 'expert'), may hold values from 0.1 to 1
- saved_gate_up: bfloat16 [4, 1024, 6, 2, 1024], P('segment', 'expert'), may hold values from -6 to 6
- w_gate_up: bfloat16 [4, 2048, 2, 32768], P('segment', None, None, 'expert'), may hold values from -0.125 to 0.125
- w_down: bfloat16 [4, 32768, 2048], P('segment', 'expert'), may hold values from -0.1875 to 0.1875
Outputs:
- forward_output: bfloat16 [4, 1024, 2048], P('segment', 'expert')
- input_grad: bfloat16 [4, 1024, 2048], P('segment', 'expert')
The draws below stay inside these ranges and needn't reach their ends.
Inputs may be any that keep to these rules, and one draw needn't show every extreme that they name: `forward_routes`: each row names 6 different experts. Among the 8 rows of one device no expert is named more than 2 times; some device names some expert exactly 2 times, and loads differ from expert to expert. `backward_routes`: each row names 6 different experts. Among the 8 rows of one device no expert is named more than 2 times; some device names some expert exactly 2 times, and loads differ from expert to expert.
All inputs are finite; a program needn't handle non-finite values.
Results may differ from the reference program's by a relative error of at most 0.007.
Values may be sent and summed in bfloat16 or wider, within the bound.
A program may use at most 64 MiB of HBM per device.

```python
import math
import jax
import jax.numpy as jnp
import numpy as np
from jax import lax

D = 2048
FF = 1024
EXPERTS = 32
TOP = 6
TOK_DEV = 8
SEGMENTS = 4
TOKENS = 1024
SPLIT = 4
CAP = 2
N_EXPERT = 128


def shard_levels(own_key, dims, split, least, largest):
    def one(dim, parts):
        steps = jax.random.uniform(jax.random.fold_in(jax.random.fold_in(own_key, 6), dim), (parts,), jnp.float32, least / len(split), largest / len(split))
        return jnp.repeat(jnp.exp(steps), dims[dim] // parts).reshape((-1,) + (1,) * (len(dims) - dim - 1))

    loudness = one(*split[0])
    for cut in split[1:]:
        loudness = loudness * one(*cut)
    return loudness


def shared_out(own_key, own, number, rows, amount, top, reach, lean):
    sequence = jax.random.permutation(own_key, amount)
    heavy_load, common = load_shares(amount, rows * top, reach, lean, True), load_shares(amount, rows * top, reach, lean, False)
    places = jnp.arange(amount)

    def named(sizes, offset_by):
        used = int((sizes > 0).sum())
        fixed = max(1, used // 4)
        moved = fixed + (places - fixed + offset_by * (used - fixed)) % max(1, amount - fixed)
        return jnp.zeros((amount,), jnp.int32).at[sequence[jnp.where(places < fixed, places, moved)]].set(jnp.asarray(sizes, jnp.int32))

    sizes = jnp.where(number % 4 == 0, named(heavy_load, number // 4), named(common, number - number // 4 - 1))
    mixed = jax.random.permutation(jax.random.fold_in(own, 3), amount)
    donor, sink = mixed[0:amount // 2 * 2:2], mixed[1:amount // 2 * 2:2]
    room = jnp.minimum(sizes[donor] - 1, reach - sizes[sink]) // 2
    room = jnp.where((donor == sequence[0]) | (sink == sequence[0]) | (sizes[sink] == 0), 0, jnp.maximum(room, 0))
    moved = jax.random.randint(jax.random.fold_in(own, 4), (amount // 2,), 0, 1 << 20) % (room + 1)
    sizes = sizes.at[donor].add(-moved).at[sink].add(moved)
    labels = jnp.searchsorted(jnp.cumsum(sizes), jnp.arange(rows * top), side="right").astype(jnp.int32)
    grid = labels.reshape(top, rows).T
    grid = grid[jax.random.permutation(jax.random.fold_in(own, 1), rows)]
    offset_by = jax.random.randint(jax.random.fold_in(own, 2), (rows, 1), 0, top)
    return jnp.take_along_axis(grid, (jnp.arange(top)[None, :] + offset_by) % top, axis=1)


def load_shares(number_of, total, bound, skew, full):
    portions = [(1 << 20) // math.isqrt(standing ** skew) + 1 for standing in range(1, number_of + 1)]
    largest = bound if full else min(bound, max(-(-total // number_of), total * portions[0] // sum(portions)))
    least = 1 if total - largest >= number_of - 1 else 0
    counts, rest = [largest] + [least] * (number_of - 1), total - largest - least * (number_of - 1)
    while rest > 0:
        movable = [i for i in range(1, number_of) if counts[i] < largest] or [i for i in range(1, number_of) if counts[i] < bound]
        pool, budget = sum([portions[i] for i in movable]), rest
        for i in movable:
            addition = min(bound - counts[i], max(1, budget * portions[i] // pool), rest)
            counts[i] = counts[i] + addition
            rest = rest - addition
    return np.array(counts)


def normal_values(rng, dims, scale, bound, split=(), held_as=jnp.bfloat16):
    result = jax.random.normal(rng, dims, jnp.float32) * scale
    if len(split) > 0:
        result = shard_levels(rng, dims, split, -0.22, 0.18) * result
    return jnp.clip(result, min=-bound, max=bound).astype(held_as)


def setup_inputs(seed: int = 0) -> dict:
    streams_of = jax.random.split(jax.random.key(seed), 10)
    forward_input = normal_values(streams_of[0], (SEGMENTS, TOKENS, D), 1.0, 6.0, ((0, 4), (1, 128)))
    forward_routes_keys = jax.random.split(jax.random.fold_in(streams_of[1], 1), SEGMENTS * TOKENS // TOK_DEV)
    forward_routes_turns = jax.random.permutation(jax.random.fold_in(streams_of[1], 3), SEGMENTS * TOKENS // TOK_DEV)
    forward_routes = jax.vmap(lambda own, number: shared_out(jax.random.fold_in(streams_of[1], 2), own, number, TOK_DEV, EXPERTS, TOP, CAP, 2))(forward_routes_keys, forward_routes_turns).reshape((SEGMENTS, TOKENS, TOP))
    forward_gates = jnp.clip(0.1 + 0.9 * jax.random.uniform(streams_of[2], (SEGMENTS, TOKENS, TOP), jnp.float32) ** shard_levels(streams_of[2], (SEGMENTS, TOKENS, TOP), ((0, 4), (1, 128)), -0.2, 0.2), 0.1, 1.0)
    backward_grad = normal_values(streams_of[3], (SEGMENTS, TOKENS, D), 1.0, 6.0, ((0, 4), (1, 128)))
    backward_routes_keys = jax.random.split(jax.random.fold_in(streams_of[4], 1), SEGMENTS * TOKENS // TOK_DEV)
    backward_routes_turns = jax.random.permutation(jax.random.fold_in(streams_of[4], 3), SEGMENTS * TOKENS // TOK_DEV)
    backward_routes = jax.vmap(lambda own, number: shared_out(jax.random.fold_in(streams_of[4], 2), own, number, TOK_DEV, EXPERTS, TOP, CAP, 2))(backward_routes_keys, backward_routes_turns).reshape((SEGMENTS, TOKENS, TOP))
    backward_gates = jnp.clip(0.1 + 0.9 * jax.random.uniform(streams_of[5], (SEGMENTS, TOKENS, TOP), jnp.float32) ** shard_levels(streams_of[5], (SEGMENTS, TOKENS, TOP), ((0, 4), (1, 128)), -0.2, 0.2), 0.1, 1.0)
    saved_gate_up = normal_values(streams_of[6], (SEGMENTS, TOKENS, TOP, 2, FF), 1.0, 6.0, ((0, 4), (1, 128)))
    w_gate_up = normal_values(streams_of[7], (SEGMENTS, D, 2, EXPERTS * FF), D ** -0.5, 0.125, ((0, 4), (3, 128)))
    w_down = normal_values(streams_of[8], (SEGMENTS, EXPERTS * FF, D), FF ** -0.5, 0.1875, ((0, 4), (1, 128)))
    return {"forward_input": forward_input, "forward_routes": forward_routes, "forward_gates": forward_gates, "backward_grad": backward_grad, "backward_routes": backward_routes, "backward_gates": backward_gates, "saved_gate_up": saved_gate_up, "w_gate_up": w_gate_up, "w_down": w_down}


def slot_positions(routes):
    blocked = routes.reshape(N_EXPERT, TOK_DEV * TOP)
    expert_ids = jnp.arange(EXPERTS, dtype=jnp.int32)
    onehot = (blocked[:, :, None] == expert_ids[None, None, :]).astype(jnp.int32)
    route_ranks = jnp.sum(jnp.cumsum(onehot, axis=1) * onehot, axis=2) - 1
    sources = jnp.arange(N_EXPERT, dtype=jnp.int32)[:, None]
    position = blocked * (N_EXPERT * CAP) + sources * CAP + route_ranks
    return position.reshape(TOKENS * TOP).astype(jnp.int32)


def route_table(position):
    route_ids = jnp.arange(TOKENS * TOP, dtype=jnp.int32)
    table = jnp.full((EXPERTS * N_EXPERT * CAP,), TOKENS * TOP, jnp.int32)
    return table.at[position].set(route_ids)


def forward_section(arrived, routes, route_gates, pair_weights, down_weights):
    position = slot_positions(routes)
    table = route_table(position)
    repeated = jnp.concatenate([jnp.repeat(arrived, TOP, axis=0), jnp.zeros((1, D), jnp.bfloat16)], axis=0)
    expert_rows = repeated[table].reshape(EXPERTS, N_EXPERT * CAP, D)
    pair_all = pair_weights.reshape(D, 2, EXPERTS, FF)
    down_all = down_weights.reshape(EXPERTS, FF, D)
    part_width = FF // SPLIT

    def one_expert(index):
        rows_here = expert_rows[index]
        gate_value = jnp.dot(rows_here, pair_all[:, 0, index], preferred_element_type=jnp.float32)
        upper_value = jnp.dot(rows_here, pair_all[:, 1, index], preferred_element_type=jnp.float32)
        hidden = (jax.nn.silu(gate_value) * upper_value).astype(jnp.bfloat16)
        down_here = down_all[index]
        total = jnp.zeros((N_EXPERT * CAP, D), jnp.float32)
        for part in range(SPLIT):
            start = part * part_width
            piece = jnp.dot(hidden[:, start:start + part_width], down_here[start:start + part_width], preferred_element_type=jnp.float32)
            total = total + piece.astype(jnp.bfloat16).astype(jnp.float32)
        return total

    summed = lax.map(one_expert, jnp.arange(EXPERTS, dtype=jnp.int32))
    per_route = summed.reshape(EXPERTS * N_EXPERT * CAP, D)[position].reshape(TOKENS, TOP, D)
    mixed = jnp.sum(per_route * route_gates[:, :, None], axis=1)
    return (arrived.astype(jnp.float32) + mixed).astype(jnp.bfloat16)


def backward_section(returning, routes, route_gates, saved, pair_weights, down_weights):
    position = slot_positions(routes)
    table = route_table(position)
    repeated = jnp.concatenate([jnp.repeat(returning, TOP, axis=0), jnp.zeros((1, D), jnp.bfloat16)], axis=0)
    grad_rows = repeated[table].reshape(EXPERTS, N_EXPERT * CAP, D)
    saved_flat = jnp.concatenate([saved.reshape(TOKENS * TOP, 2, FF), jnp.zeros((1, 2, FF), jnp.bfloat16)], axis=0)
    pair_rows = saved_flat[table].reshape(EXPERTS, N_EXPERT * CAP, 2, FF)
    pair_all = pair_weights.reshape(D, 2, EXPERTS, FF)
    down_all = down_weights.reshape(EXPERTS, FF, D)
    part_width = FF // SPLIT

    def one_expert(index):
        grads_here = grad_rows[index]
        pairs_here = pair_rows[index].astype(jnp.float32)
        grad_hidden = jnp.dot(grads_here, down_all[index].T, preferred_element_type=jnp.float32)
        gate_value = pairs_here[:, 0]
        upper_value = pairs_here[:, 1]
        sigmoid_gate = jax.nn.sigmoid(gate_value)
        grad_gate = (grad_hidden * upper_value * sigmoid_gate * (1.0 + gate_value * (1.0 - sigmoid_gate))).astype(jnp.bfloat16)
        grad_upper = (grad_hidden * jax.nn.silu(gate_value)).astype(jnp.bfloat16)
        gate_weights = pair_all[:, 0, index]
        upper_weights = pair_all[:, 1, index]
        total = jnp.zeros((N_EXPERT * CAP, D), jnp.float32)
        for part in range(SPLIT):
            start = part * part_width
            term = jnp.dot(grad_gate[:, start:start + part_width], gate_weights[:, start:start + part_width].T, preferred_element_type=jnp.float32)
            term = term + jnp.dot(grad_upper[:, start:start + part_width], upper_weights[:, start:start + part_width].T, preferred_element_type=jnp.float32)
            total = total + term.astype(jnp.bfloat16).astype(jnp.float32)
        return total

    summed = lax.map(one_expert, jnp.arange(EXPERTS, dtype=jnp.int32))
    per_route = summed.reshape(EXPERTS * N_EXPERT * CAP, D)[position].reshape(TOKENS, TOP, D)
    mixed = jnp.sum(per_route * route_gates[:, :, None], axis=1)
    return (returning.astype(jnp.float32) + mixed).astype(jnp.bfloat16)


def reference(forward_input, forward_routes, forward_gates, backward_grad, backward_routes, backward_gates, saved_gate_up, w_gate_up, w_down):
    outputs = []
    gradients = []
    for section in range(SEGMENTS):
        arrived = forward_input[(section - 1) % SEGMENTS]
        returning = backward_grad[(section + 1) % SEGMENTS]
        outputs.append(forward_section(arrived, forward_routes[section], forward_gates[section], w_gate_up[section], w_down[section]))
        gradients.append(backward_section(returning, backward_routes[section], backward_gates[section], saved_gate_up[section], w_gate_up[section], w_down[section]))
    return jnp.stack(outputs), jnp.stack(gradients)
```

```python
import functools

import jax
import jax.numpy as jnp
from jax import lax
from jax.experimental import pallas as pl
from jax.experimental.pallas import tpu as pltpu
from jax.sharding import PartitionSpec as P

CAP = 2
PARTS = 4
LANES = 128
MESH = pl.DeviceIdType.MESH
F32 = jnp.float32
BF16 = jnp.bfloat16


def on_chip(
    groups, sections,
    fwd_ref, froute_ref, fgate_ref, bwd_ref, broute_ref, bgate_ref, saved_ref, wgu_ref, wd_ref,
    out_f, out_b,
    stage, landed, snd, rcv, wide, rows_f, rows_b, rows_p, pairs, part_f, part_b,
    sib_f, sib_b, pass_f, pass_b, near_f, near_b, home_snd, home_rcv,
    shift_s, shift_r, a2a_s, a2a_r, quad_s, quad_r, pair_s, pair_r, red_s, red_r,
):
    seg = lax.axis_index("segment")
    idx = lax.axis_index("expert")
    e = idx // PARTS
    q = idx % PARTS
    xl = q // 2
    c = q % 2
    sib_q = xl * 2 + (1 - c)
    near_q = (1 - xl) * 2 + c
    sib = (seg, e * PARTS + sib_q)
    near = (seg, e * PARTS + near_q)
    slots = CAP * groups
    width = wd_ref.shape[1]
    part = wd_ref.shape[0]
    tokens, top = froute_ref.shape
    blocks = width // LANES
    chunk = CAP * blocks

    def remote(src, dst, ss, rs, where):
        return pltpu.make_async_remote_copy(
            src_ref=src, dst_ref=dst, send_sem=ss, recv_sem=rs, device_id=where, device_id_type=MESH
        )

    half = width // 2
    for i, ref in enumerate((fwd_ref, bwd_ref)):
        v = ref[...].astype(F32)
        stage[i] = jnp.concatenate([v[:, :half], v[:, half:]], axis=0).astype(BF16)

    barrier = pltpu.get_barrier_semaphore()

    @pl.loop(1, groups)
    def _(i):
        pl.semaphore_signal(barrier, inc=1, device_id=(seg, (e + i) % groups * PARTS + q), device_id_type=MESH)

    for i in range(1, PARTS):
        pl.semaphore_signal(barrier, inc=1, device_id=(seg, e * PARTS + (q + i) % PARTS), device_id_type=MESH)
    after = (seg + 1) % sections
    before = (seg + sections - 1) % sections
    for there in (after, before):
        pl.semaphore_signal(barrier, inc=1, device_id=(there, idx), device_id_type=MESH)
    pl.semaphore_wait(barrier, groups + PARTS)

    shifts = [
        remote(stage.at[i], landed.at[i], shift_s.at[i], shift_r.at[i], (there, idx))
        for i, there in enumerate((after, before))
    ]
    for s in shifts:
        s.start()

    lane = lax.broadcasted_iota(jnp.int32, (tokens, slots), 1)
    lane_e = lane // CAP
    lane_c = (lane % CAP).astype(F32)
    earlier = (
        lax.broadcasted_iota(jnp.int32, (tokens, tokens), 1) < lax.broadcasted_iota(jnp.int32, (tokens, tokens), 0)
    ).astype(F32)

    def matches(route_ref, gate_ref):
        hits = [(route_ref[:, k:k + 1] == lane_e).astype(F32) for k in range(top)]
        named = functools.reduce(jnp.add, hits)
        rank = jnp.dot(earlier, named, preferred_element_type=F32)
        sel = jnp.where(rank == lane_c, named, 0.0)
        weight = functools.reduce(jnp.add, [hits[k] * gate_ref[:, k:k + 1] for k in range(top)]) * sel
        return hits, sel, weight

    fhits, fsel, fweight = matches(froute_ref, fgate_ref)
    bhits, bsel, bweight = matches(broute_ref, bgate_ref)
    psel = jnp.concatenate([h * bsel for h in bhits], axis=0)

    def pick(sel, rows):
        return lax.dot_general(
            sel.T.astype(BF16), rows, (((1,), (0,)), ((), ())), preferred_element_type=F32
        )

    def to_chunks(values, out):
        for b in range(blocks):
            wide[pl.ds(b, slots, stride=blocks), :] = values[:, b * LANES:(b + 1) * LANES]
        out[...] = wide[...].astype(BF16)

    def to_rows(ref):
        wide[...] = ref[...].astype(F32)
        return jnp.concatenate([wide[pl.ds(b, slots, stride=blocks), :] for b in range(blocks)], axis=1)

    def exchange(send, recv, ss, rs):
        own = pl.ds(pl.multiple_of(e * chunk, chunk), chunk)

        @pl.loop(1, groups)
        def _(i):
            there = (e + i) % groups
            remote(
                send.at[pl.ds(pl.multiple_of(there * chunk, chunk), chunk)], recv.at[own], ss, rs,
                (seg, there * PARTS + q),
            ).start()

        recv[own, :] = send[own, :]

    def all_of(send, recv, ss, rs):
        n = (groups - 1) * chunk
        return remote(send.at[pl.ds(0, n)], recv.at[pl.ds(0, n)], ss, rs, sib)

    ROWS = lambda k: pl.ds(pl.multiple_of(k * slots, slots), slots)

    to_chunks(pick(psel, saved_ref[...]), snd.at[2])
    exchange(snd.at[2], rcv.at[2], a2a_s.at[2], a2a_r.at[2])

    def unstaged(i):
        shifts[i].wait_recv()
        v = landed[i].astype(F32)
        return jnp.concatenate([v[:tokens], v[tokens:]], axis=1)

    arrived = unstaged(0)
    to_chunks(pick(fsel, arrived.astype(BF16)), snd.at[0])
    exchange(snd.at[0], rcv.at[0], a2a_s.at[0], a2a_r.at[0])
    returning = unstaged(1)
    to_chunks(pick(bsel, returning.astype(BF16)), snd.at[1])
    exchange(snd.at[1], rcv.at[1], a2a_s.at[1], a2a_r.at[1])

    def share_out(d, rows):
        all_of(snd.at[d], rcv.at[d], a2a_s.at[d], a2a_r.at[d]).wait_recv()
        rows[ROWS(q), :] = to_rows(rcv.at[d]).astype(BF16)
        to_near = remote(rows.at[ROWS(q)], rows.at[ROWS(q)], quad_s.at[d, 0], quad_r.at[d, 0], near)
        to_sib = remote(rows.at[ROWS(q)], rows.at[ROWS(q)], quad_s.at[d, 1], quad_r.at[d, 1], sib)
        to_near.start()
        to_sib.start()
        return to_near, to_sib

    def hand_on(d, rows, to_near):
        to_near.wait_recv()
        on = remote(rows.at[ROWS(near_q)], rows.at[ROWS(near_q)], quad_s.at[d, 2], quad_r.at[d, 2], sib)
        on.start()
        return on

    f_near, f_sib = share_out(0, rows_f)

    all_of(snd.at[2], rcv.at[2], a2a_s.at[2], a2a_r.at[2]).wait_recv()
    rows_p[...] = to_rows(rcv.at[2]).astype(BF16)
    pair_copies = []
    for i in range(1, PARTS):
        there = (q + i) % PARTS
        for g in range(2):
            pair_copies.append(
                remote(
                    rows_p.at[:, pl.ds(pl.multiple_of((g * PARTS + there) * part, part), part)],
                    pairs.at[ROWS(q), pl.ds(g * part, part)],
                    pair_s.at[i - 1, g], pair_r.at[i - 1, g], (seg, e * PARTS + there),
                )
            )
            pair_copies[-1].start()
    for g in range(2):
        pairs[ROWS(q), pl.ds(g * part, part)] = rows_p[
            :, pl.ds(pl.multiple_of((g * PARTS + q) * part, part), part)
        ]

    f_on = hand_on(0, rows_f, f_near)
    b_near, b_sib = share_out(1, rows_b)

    f_sib.wait_recv()
    f_on.wait_recv()
    both = jnp.dot(rows_f[...], wgu_ref[...], preferred_element_type=F32)
    gate = both[:, :part]
    hidden = (gate / (1.0 + jnp.exp(-gate)) * both[:, part:]).astype(BF16)
    part_f[...] = jnp.dot(hidden, wd_ref[...], preferred_element_type=F32).astype(BF16)

    def sum_sib(d, parts, from_sib):
        copies = []
        for x in range(2):
            copies.append(
                remote(parts.at[ROWS(x * 2 + 1 - c)], from_sib.at[x], red_s.at[d, x], red_r.at[d, x], sib)
            )
            copies[-1].start()
        return copies

    f_red = sum_sib(0, part_f, sib_f)
    b_on = hand_on(1, rows_b, b_near)

    def sum_near(d, parts, from_sib, passed, from_near, copies):
        for one in copies:
            one.wait_recv()
        passed[...] = (parts[ROWS(near_q), :].astype(F32) + from_sib[1 - xl].astype(F32)).astype(BF16)
        one = remote(passed, from_near, red_s.at[d, 2], red_r.at[d, 2], near)
        one.start()
        return one

    f_pass = sum_near(0, part_f, sib_f, pass_f, near_f, f_red)

    b_sib.wait_recv()
    b_on.wait_recv()
    for one in pair_copies:
        one.wait_recv()
    grad_hidden = lax.dot_general(rows_b[...], wd_ref[...], (((1,), (1,)), ((), ())), preferred_element_type=F32)
    a = pairs[:, :part].astype(F32)
    b = pairs[:, part:].astype(F32)
    sig = 1.0 / (1.0 + jnp.exp(-a))
    grad_gate = (grad_hidden * b * sig * (1.0 + a * (1.0 - sig))).astype(BF16)
    grad_upper = (grad_hidden * (a * sig)).astype(BF16)
    both_grads = jnp.concatenate([grad_gate, grad_upper], axis=1)
    part_b[...] = lax.dot_general(
        both_grads, wgu_ref[...], (((1,), (1,)), ((), ())), preferred_element_type=F32
    ).astype(BF16)
    b_red = sum_sib(1, part_b, sib_b)

    def go_home(d, parts, from_sib, from_near, copy):
        copy.wait_recv()
        total = parts[ROWS(q), :].astype(F32) + from_sib[xl].astype(F32) + from_near[...].astype(F32)
        to_chunks(total, home_snd.at[d])
        exchange(home_snd.at[d], home_rcv.at[d], a2a_s.at[3 + d], a2a_r.at[3 + d])

    go_home(0, part_f, sib_f, near_f, f_pass)
    b_pass = sum_near(1, part_b, sib_b, pass_b, near_b, b_red)
    go_home(1, part_b, sib_b, near_b, b_pass)

    def finish(d, weight, residual, out):
        all_of(home_snd.at[d], home_rcv.at[d], a2a_s.at[3 + d], a2a_r.at[3 + d]).wait_recv()
        rows = to_rows(home_rcv.at[d]).astype(BF16)
        high = weight.astype(BF16)
        low = (weight - high.astype(F32)).astype(BF16)
        mixed = jnp.dot(high, rows, preferred_element_type=F32) + jnp.dot(low, rows, preferred_element_type=F32)
        out[...] = (residual + mixed).astype(BF16)

    finish(0, fweight, arrived, out_f)
    finish(1, bweight, returning, out_b)

    for s in (*shifts, f_near, f_sib, f_on, b_near, b_sib, b_on, *pair_copies, *f_red, *b_red, f_pass, b_pass):
        s.wait_send()
    for d in range(3):
        all_of(snd.at[d], rcv.at[d], a2a_s.at[d], a2a_r.at[d]).wait_send()
    for d in range(2):
        all_of(home_snd.at[d], home_rcv.at[d], a2a_s.at[3 + d], a2a_r.at[3 + d]).wait_send()


def on_device(
    groups, sections,
    forward_input, forward_routes, forward_gates, backward_grad, backward_routes, backward_gates,
    saved_gate_up, w_gate_up, w_down,
):
    _, tokens, width = forward_input.shape
    top = forward_routes.shape[-1]
    hidden = saved_gate_up.shape[-1]
    part = w_down.shape[1]
    slots = CAP * groups
    saved = jnp.transpose(saved_gate_up[0], (1, 0, 2, 3)).reshape(top * tokens, 2 * hidden)
    wgu = w_gate_up[0].reshape(width, 2 * part)
    vmem = pl.BlockSpec(memory_space=pltpu.VMEM)
    long = slots * width // LANES
    row = jax.ShapeDtypeStruct((tokens, width), BF16)
    dma = pltpu.SemaphoreType.DMA
    out_f, out_b = pl.pallas_call(
        functools.partial(on_chip, groups, sections),
        out_shape=(row, row),
        in_specs=[vmem] * 9,
        out_specs=(vmem, vmem),
        scratch_shapes=[
            pltpu.VMEM((2, 2 * tokens, width // 2), BF16),
            pltpu.VMEM((2, 2 * tokens, width // 2), BF16),
            pltpu.VMEM((3, long, LANES), BF16),
            pltpu.VMEM((3, long, LANES), BF16),
            pltpu.VMEM((long, LANES), F32),
            pltpu.VMEM((PARTS * slots, width), BF16),
            pltpu.VMEM((PARTS * slots, width), BF16),
            pltpu.VMEM((slots, 2 * hidden), BF16),
            pltpu.VMEM((PARTS * slots, 2 * part), BF16),
            pltpu.VMEM((PARTS * slots, width), BF16),
            pltpu.VMEM((PARTS * slots, width), BF16),
            pltpu.VMEM((2, slots, width), BF16),
            pltpu.VMEM((2, slots, width), BF16),
            pltpu.VMEM((slots, width), BF16),
            pltpu.VMEM((slots, width), BF16),
            pltpu.VMEM((slots, width), BF16),
            pltpu.VMEM((slots, width), BF16),
            pltpu.VMEM((2, long, LANES), BF16),
            pltpu.VMEM((2, long, LANES), BF16),
            dma((2,)), dma((2,)), dma((5,)), dma((5,)), dma((2, 3)), dma((2, 3)),
            dma((PARTS - 1, 2)), dma((PARTS - 1, 2)), dma((2, 3)), dma((2, 3)),
        ],
        compiler_params=pltpu.CompilerParams(
            collective_id=0, has_side_effects=True, vmem_limit_bytes=40 * 2**20
        ),
    )(
        forward_input[0], forward_routes[0], forward_gates[0], backward_grad[0], backward_routes[0],
        backward_gates[0], saved, wgu, w_down[0],
    )
    return out_f[None], out_b[None]


def solution(mesh):
    spec = P("segment", "expert", None)
    placed = (
        spec, spec, spec, spec, spec, spec,
        P("segment", "expert", None, None, None),
        P("segment", None, None, "expert"),
        spec,
    )
    return jax.shard_map(
        functools.partial(on_device, mesh.shape["expert"] // PARTS, mesh.shape["segment"]),
        mesh=mesh,
        in_specs=placed,
        out_specs=(spec, spec),
        check_vma=False,
    )
```

```python
import functools

import jax
import jax.numpy as jnp
from jax import lax
from jax.experimental import pallas as pl
from jax.experimental.pallas import tpu as pltpu
from jax.sharding import PartitionSpec as P

CAP = 2
PARTS = 4
LANES = 128
MESH = pl.DeviceIdType.MESH
F32 = jnp.float32
BF16 = jnp.bfloat16


def on_chip(
    groups, sections,
    fwd_hbm, bwd_hbm, froute_hbm, fgate_hbm, broute_hbm, bgate_hbm, saved_hbm, wgu_hbm, wd_hbm,
    out_f, out_b,
    fwd_ref, bwd_ref, froute_ref, fgate_ref, broute_ref, bgate_ref, saved_ref, wgu_raw, wd_ref,
    stage, landed, wgu_ref, saved_rows, wide,
    snd, rcv, rows, pair_rows, pairs, parts, from_sib, passed, from_near, home_snd, home_rcv,
    load_s, shift_s, shift_r, a2a_s, a2a_r, quad_s, quad_r, pair_s, pair_r, red_s, red_r,
):
    seg = lax.axis_index("segment")
    idx = lax.axis_index("expert")
    e = idx // PARTS
    q = idx % PARTS
    xl = q // 2
    c = q % 2
    near_q = (1 - xl) * 2 + c
    sib = (seg, e * PARTS + xl * 2 + (1 - c))
    near = (seg, e * PARTS + near_q)
    width = wd_ref.shape[1]
    part = wd_ref.shape[0]
    top, _, tokens = froute_ref.shape
    blocks = width // LANES
    half = width // 2
    sent = []

    def remote(src, dst, ss, rs, where):
        return pltpu.make_async_remote_copy(
            src_ref=src, dst_ref=dst, send_sem=ss, recv_sem=rs, device_id=where, device_id_type=MESH
        )

    def send(*what):
        copy = remote(*what)
        copy.start()
        sent.append(copy)
        return copy

    def peer(there):
        return (seg, there * PARTS + (q + 2 * ((e + there) % 2)) % PARTS)

    loads = [
        pltpu.make_async_copy(there, here, load_s.at[i])
        for i, (there, here) in enumerate((
            (fwd_hbm, fwd_ref), (bwd_hbm, bwd_ref), (froute_hbm, froute_ref), (fgate_hbm, fgate_ref),
            (broute_hbm, broute_ref), (bgate_hbm, bgate_ref), (saved_hbm, saved_ref), (wgu_hbm, wgu_raw),
            (wd_hbm, wd_ref),
        ))
    ]
    for one in loads:
        one.start()

    barrier = pltpu.get_barrier_semaphore()

    @pl.loop(1, groups)
    def _(i):
        pl.semaphore_signal(barrier, inc=1, device_id=peer((e + i) % groups), device_id_type=MESH)

    for i in range(1, PARTS):
        pl.semaphore_signal(barrier, inc=1, device_id=(seg, e * PARTS + (q + i) % PARTS), device_id_type=MESH)
    after = (seg + 1) % sections
    before = (seg + sections - 1) % sections
    for there in (after, before):
        pl.semaphore_signal(barrier, inc=1, device_id=(there, idx), device_id_type=MESH)

    for i, ref in enumerate((fwd_ref, bwd_ref)):
        loads[i].wait()
        v = ref[...].astype(F32)
        stage[i] = jnp.concatenate([v[:, :half], v[:, half:]], axis=0).astype(BF16)

    pl.semaphore_wait(barrier, groups + PARTS)
    shifts = [
        send(stage.at[i], landed.at[i], shift_s.at[i], shift_r.at[i], (there, idx))
        for i, there in enumerate((after, before))
    ]

    for one in loads[2:7]:
        one.wait()
    for g in range(2):
        saved_rows[:, g * half:(g + 1) * half] = saved_ref[:, g, :]

    row_e = lax.broadcasted_iota(jnp.int32, (groups, tokens), 0)
    prior = (
        lax.broadcasted_iota(jnp.int32, (tokens, tokens), 0) < lax.broadcasted_iota(jnp.int32, (tokens, tokens), 1)
    ).astype(F32)

    def matches(route_ref, gate_ref):
        hits = [(row_e == route_ref[k]).astype(F32) for k in range(top)]
        named = functools.reduce(jnp.add, hits)
        rank = jnp.dot(named, prior, preferred_element_type=F32)
        gate = functools.reduce(jnp.add, [hits[k] * gate_ref[k] for k in range(top)])
        sels = [jnp.where(rank == float(h), named, 0.0) for h in range(CAP)]
        return hits, sels, [(gate * s).T for s in sels]

    bhits, bsels, bweights = matches(broute_ref, bgate_ref)
    fhits, fsels, fweights = matches(froute_ref, fgate_ref)
    n = top * tokens
    kt = lax.broadcasted_iota(jnp.int32, (n, n), 0)
    tk = lax.broadcasted_iota(jnp.int32, (n, n), 1)
    turn = ((kt % tokens) * top + kt // tokens == tk).astype(F32)
    psels = [
        jnp.dot(jnp.concatenate([h * s for h in bhits], axis=1), turn, preferred_element_type=F32) for s in bsels
    ]

    def pick(sel, values):
        return jnp.dot(sel.astype(BF16), values, preferred_element_type=F32)

    def to_chunks(values, out):
        for b in range(blocks):
            wide[pl.ds(b, groups, stride=blocks), :] = values[:, b * LANES:(b + 1) * LANES]
        out[...] = wide[...].astype(BF16)

    def to_rows(ref):
        wide[...] = ref[...].astype(F32)
        return jnp.concatenate(
            [wide[pl.ds(b, groups, stride=blocks), :].astype(BF16) for b in range(blocks)], axis=1
        )

    span = (groups - 1) * blocks

    def exchange(src, dst, s):
        own = pl.ds(pl.multiple_of(e * blocks, blocks), blocks)

        @pl.loop(1, groups)
        def _(i):
            there = (e + i) % groups
            remote(
                src.at[pl.ds(pl.multiple_of(there * blocks, blocks), blocks)], dst.at[own],
                a2a_s.at[s], a2a_r.at[s], peer(there),
            ).start()

        dst[own, :] = src[own, :]
        whole = remote(src.at[pl.ds(0, span)], dst.at[pl.ds(0, span)], a2a_s.at[s], a2a_r.at[s], sib)
        sent.append(whole)
        return whole

    def ROWS(k):
        return pl.ds(pl.multiple_of(k * groups, groups), groups)

    came, shares, ons, sibs, passes, homes, pair_copies = {}, {}, {}, {}, {}, {}, {}

    def dispatch(u, sel, values):
        to_chunks(pick(sel, values), snd.at[u])
        came[u] = exchange(snd.at[u], rcv.at[u], u)

    def share_out(u):
        came[u].wait_recv()
        mine = rows.at[u, ROWS(q)]
        mine[...] = to_rows(rcv.at[u])
        shares[u] = (
            send(mine, mine, quad_s.at[u, 0], quad_r.at[u, 0], near),
            send(mine, mine, quad_s.at[u, 1], quad_r.at[u, 1], sib),
        )

    def hand_on(u):
        shares[u][0].wait_recv()
        other = rows.at[u, ROWS(near_q)]
        ons[u] = send(other, other, quad_s.at[u, 2], quad_r.at[u, 2], sib)

    def share_pairs(h):
        came[4 + h].wait_recv()
        pair_rows[h] = to_rows(rcv.at[4 + h])
        cols = [
            [pl.ds(pl.multiple_of((g * PARTS + (q + i) % PARTS) * part, part), part) for g in range(2)]
            for i in range(PARTS)
        ]
        pair_copies[h] = [
            send(
                pair_rows.at[h, :, cols[i][g]], pairs.at[h, ROWS(q), pl.ds(g * part, part)],
                pair_s.at[h, i - 1, g], pair_r.at[h, i - 1, g], (seg, e * PARTS + (q + i) % PARTS),
            )
            for i in range(1, PARTS)
            for g in range(2)
        ]
        for g in range(2):
            pairs[h, ROWS(q), g * part:(g + 1) * part] = pair_rows[h, :, cols[0][g]]

    def compute(u):
        shares[u][1].wait_recv()
        ons[u].wait_recv()
        if u < CAP:
            both = jnp.dot(rows[u], wgu_ref[...], preferred_element_type=F32)
            gate = both[:, :part]
            hidden = (gate / (1.0 + jnp.exp(-gate)) * both[:, part:]).astype(BF16)
            parts[u] = jnp.dot(hidden, wd_ref[...], preferred_element_type=F32).astype(BF16)
        else:
            h = u - CAP
            for one in pair_copies[h]:
                one.wait_recv()
            grad_hidden = lax.dot_general(
                rows[u], wd_ref[...], (((1,), (1,)), ((), ())), preferred_element_type=F32
            )
            a = pairs[h, :, :part].astype(F32)
            b = pairs[h, :, part:].astype(F32)
            sig = 1.0 / (1.0 + jnp.exp(-a))
            grad_gate = (grad_hidden * b * sig * (1.0 + a * (1.0 - sig))).astype(BF16)
            grad_upper = (grad_hidden * (a * sig)).astype(BF16)
            parts[u] = lax.dot_general(
                jnp.concatenate([grad_gate, grad_upper], axis=1), wgu_ref[...],
                (((1,), (1,)), ((), ())), preferred_element_type=F32,
            ).astype(BF16)
        sibs[u] = [
            send(parts.at[u, ROWS(x * 2 + 1 - c)], from_sib.at[u, x], red_s.at[u, x], red_r.at[u, x], sib)
            for x in range(2)
        ]

    def sum_core(u):
        for one in sibs[u]:
            one.wait_recv()
        passed[u] = (parts[u, ROWS(near_q), :].astype(F32) + from_sib[u, 1 - xl].astype(F32)).astype(BF16)
        passes[u] = send(passed.at[u], from_near.at[u], red_s.at[u, 2], red_r.at[u, 2], near)

    def go_home(u):
        passes[u].wait_recv()
        total = parts[u, ROWS(q), :].astype(F32) + from_sib[u, xl].astype(F32) + from_near[u].astype(F32)
        to_chunks(total, home_snd.at[u])
        homes[u] = exchange(home_snd.at[u], home_rcv.at[u], 6 + u)

    def combined(u, weight):
        homes[u].wait_recv()
        back = to_rows(home_rcv.at[u])
        high = weight.astype(BF16)
        low = (weight - high.astype(F32)).astype(BF16)
        return jnp.dot(high, back, preferred_element_type=F32) + jnp.dot(low, back, preferred_element_type=F32)

    def unstaged(i):
        shifts[i].wait_recv()
        v = landed[i].astype(F32)
        return jnp.concatenate([v[:tokens], v[tokens:]], axis=1)

    steps = 8
    step = width // steps

    def lay_out(first, last):
        @pl.loop(first, last)
        def _(i):
            some = pl.ds(pl.multiple_of(i * step, step), step)
            for g in range(2):
                wgu_ref[some, g * part:(g + 1) * part] = wgu_raw[some, g, :]

    arrived = unstaged(0)
    dispatch(0, fsels[0], arrived.astype(BF16))
    dispatch(4, psels[0], saved_rows[...])
    dispatch(1, fsels[1], arrived.astype(BF16))
    returning = unstaged(1)
    dispatch(2, bsels[0], returning.astype(BF16))
    for one in loads[7:]:
        one.wait()
    lay_out(0, steps)
    share_out(0)
    share_pairs(0)
    dispatch(5, psels[1], saved_rows[...])
    dispatch(3, bsels[1], returning.astype(BF16))
    share_out(1)
    hand_on(0)
    share_out(2)
    compute(0)
    hand_on(1)
    sum_core(0)
    share_pairs(1)
    compute(1)
    hand_on(2)
    sum_core(1)
    share_out(3)
    compute(2)
    go_home(0)
    sum_core(2)
    go_home(1)
    hand_on(3)
    compute(3)
    go_home(2)
    sum_core(3)
    mixed_f = combined(0, fweights[0])
    go_home(3)
    out_f[...] = (arrived + mixed_f + combined(1, fweights[1])).astype(BF16)
    mixed_b = combined(2, bweights[0])
    out_b[...] = (returning + mixed_b + combined(3, bweights[1])).astype(BF16)

    for one in sent:
        one.wait_send()


def on_device(
    groups, sections,
    forward_input, forward_routes, forward_gates, backward_grad, backward_routes, backward_gates,
    saved_gate_up, w_gate_up, w_down,
):
    _, tokens, width = forward_input.shape
    top = forward_routes.shape[-1]
    hidden = saved_gate_up.shape[-1]
    part = w_down.shape[1]
    hbm = pl.BlockSpec(memory_space=pl.ANY)
    long = groups * width // LANES
    row = jax.ShapeDtypeStruct((tokens, width), BF16)
    dma = pltpu.SemaphoreType.DMA
    units = 2 * CAP
    by_top = lambda v: jnp.transpose(v, (2, 0, 1))
    out_f, out_b = pl.pallas_call(
        functools.partial(on_chip, groups, sections),
        out_shape=(row, row),
        in_specs=[hbm] * 9,
        out_specs=(pl.BlockSpec(memory_space=pltpu.VMEM),) * 2,
        scratch_shapes=[
            pltpu.VMEM((tokens, width), BF16),
            pltpu.VMEM((tokens, width), BF16),
            pltpu.VMEM((top, 1, tokens), jnp.int32),
            pltpu.VMEM((top, 1, tokens), F32),
            pltpu.VMEM((top, 1, tokens), jnp.int32),
            pltpu.VMEM((top, 1, tokens), F32),
            pltpu.VMEM((tokens * top, 2, hidden), BF16),
            pltpu.VMEM((width, 2, part), BF16),
            pltpu.VMEM((part, width), BF16),
            pltpu.VMEM((2, 2 * tokens, width // 2), BF16),
            pltpu.VMEM((2, 2 * tokens, width // 2), BF16),
            pltpu.VMEM((width, 2 * part), BF16),
            pltpu.VMEM((tokens * top, 2 * hidden), BF16),
            pltpu.VMEM((long, LANES), F32),
            pltpu.VMEM((units + CAP, long, LANES), BF16),
            pltpu.VMEM((units + CAP, long, LANES), BF16),
            pltpu.VMEM((units, PARTS * groups, width), BF16),
            pltpu.VMEM((CAP, groups, 2 * hidden), BF16),
            pltpu.VMEM((CAP, PARTS * groups, 2 * part), BF16),
            pltpu.VMEM((units, PARTS * groups, width), BF16),
            pltpu.VMEM((units, 2, groups, width), BF16),
            pltpu.VMEM((units, groups, width), BF16),
            pltpu.VMEM((units, groups, width), BF16),
            pltpu.VMEM((units, long, LANES), BF16),
            pltpu.VMEM((units, long, LANES), BF16),
            dma((9,)), dma((2,)), dma((2,)),
            dma((2 * units + CAP,)), dma((2 * units + CAP,)), dma((units, 3)), dma((units, 3)),
            dma((CAP, PARTS - 1, 2)), dma((CAP, PARTS - 1, 2)), dma((units, 3)), dma((units, 3)),
        ],
        compiler_params=pltpu.CompilerParams(
            collective_id=0, has_side_effects=True, vmem_limit_bytes=62 * 2**20
        ),
    )(
        forward_input[0], backward_grad[0], by_top(forward_routes), by_top(forward_gates),
        by_top(backward_routes), by_top(backward_gates),
        saved_gate_up[0].reshape(tokens * top, 2, hidden), w_gate_up[0], w_down[0],
    )
    return out_f[None], out_b[None]


def solution(mesh):
    spec = P("segment", "expert", None)
    placed = (
        spec, spec, spec, spec, spec, spec,
        P("segment", "expert", None, None, None),
        P("segment", None, None, "expert"),
        spec,
    )
    return jax.shard_map(
        functools.partial(on_device, mesh.shape["expert"] // PARTS, mesh.shape["segment"]),
        mesh=mesh,
        in_specs=placed,
        out_specs=(spec, spec),
        check_vma=False,
    )
```

```python
import functools

import jax
import jax.numpy as jnp
from jax import lax
from jax.experimental import pallas as pl
from jax.experimental.pallas import tpu as pltpu
from jax.sharding import PartitionSpec as P

CAP = 2
PARTS = 4
LANES = 128
MESH = pl.DeviceIdType.MESH
F32 = jnp.float32
BF16 = jnp.bfloat16


def on_chip(
    groups, sections,
    fwd_hbm, bwd_hbm, froute_hbm, fgate_hbm, broute_hbm, bgate_hbm, saved_hbm, wgu_hbm, wd_hbm,
    out,
    fwd_ref, bwd_ref, froute_ref, fgate_ref, broute_ref, bgate_ref, saved_ref, wgu_raw, wd_ref,
    stage, landed, wgu_ref, saved_rows, wide,
    snd, rcv, rows, pair_rows, pairs, parts, from_sib, passed, from_near, home_snd, home_rcv,
    load_s, shift_s, shift_r, a2a_s, a2a_r, quad_s, quad_r, pair_s, pair_r, red_s, red_r,
):
    seg = lax.axis_index("segment")
    idx = lax.axis_index("expert")
    e = idx // PARTS
    q = idx % PARTS
    xl = q // 2
    c = q % 2
    near_q = (1 - xl) * 2 + c
    sib = (seg, e * PARTS + xl * 2 + (1 - c))
    near = (seg, e * PARTS + near_q)
    width = wd_ref.shape[1]
    part = wd_ref.shape[0]
    top, _, tokens = froute_ref.shape
    blocks = width // LANES
    half = width // 2
    sent = []

    def remote(src, dst, ss, rs, where):
        return pltpu.make_async_remote_copy(
            src_ref=src, dst_ref=dst, send_sem=ss, recv_sem=rs, device_id=where, device_id_type=MESH
        )

    def send(*what):
        copy = remote(*what)
        copy.start()
        sent.append(copy)
        return copy

    def peer(there):
        return (seg, there * PARTS + (q + 2 * ((e + there) % 2)) % PARTS)

    loads = [
        pltpu.make_async_copy(there, here, load_s.at[i])
        for i, (there, here) in enumerate((
            (fwd_hbm, fwd_ref), (bwd_hbm, bwd_ref), (froute_hbm, froute_ref), (fgate_hbm, fgate_ref),
            (broute_hbm, broute_ref), (bgate_hbm, bgate_ref), (saved_hbm, saved_ref), (wgu_hbm, wgu_raw),
            (wd_hbm, wd_ref),
        ))
    ]
    for one in loads:
        one.start()

    barrier = pltpu.get_barrier_semaphore()

    @pl.loop(1, groups)
    def _(i):
        pl.semaphore_signal(barrier, inc=1, device_id=peer((e + i) % groups), device_id_type=MESH)

    for i in range(1, PARTS):
        pl.semaphore_signal(barrier, inc=1, device_id=(seg, e * PARTS + (q + i) % PARTS), device_id_type=MESH)
    after = (seg + 1) % sections
    before = (seg + sections - 1) % sections
    for there in (after, before):
        pl.semaphore_signal(barrier, inc=1, device_id=(there, idx), device_id_type=MESH)

    for i, ref in enumerate((fwd_ref, bwd_ref)):
        loads[i].wait()
        v = ref[...].astype(F32)
        stage[i] = jnp.concatenate([v[:, :half], v[:, half:]], axis=0).astype(BF16)

    pl.semaphore_wait(barrier, groups + PARTS)
    shifts = [
        send(stage.at[i], landed.at[i], shift_s.at[i], shift_r.at[i], (there, idx))
        for i, there in enumerate((after, before))
    ]

    for one in loads[2:7]:
        one.wait()
    for g in range(2):
        saved_rows[:, g * half:(g + 1) * half] = saved_ref[:, g, :]

    row_e = lax.broadcasted_iota(jnp.int32, (groups, tokens), 0)
    prior = (
        lax.broadcasted_iota(jnp.int32, (tokens, tokens), 0) < lax.broadcasted_iota(jnp.int32, (tokens, tokens), 1)
    ).astype(F32)

    def matches(route_ref, gate_ref):
        hits = [(row_e == route_ref[k]).astype(F32) for k in range(top)]
        named = functools.reduce(jnp.add, hits)
        rank = jnp.dot(named, prior, preferred_element_type=F32)
        gate = functools.reduce(jnp.add, [hits[k] * gate_ref[k] for k in range(top)])
        sels = [jnp.where(rank == float(h), named, 0.0) for h in range(CAP)]
        return hits, sels, [(gate * s).T for s in sels]

    bhits, bsels, bweights = matches(broute_ref, bgate_ref)
    fhits, fsels, fweights = matches(froute_ref, fgate_ref)
    n = top * tokens
    kt = lax.broadcasted_iota(jnp.int32, (n, n), 0)
    tk = lax.broadcasted_iota(jnp.int32, (n, n), 1)
    turn = ((kt % tokens) * top + kt // tokens == tk).astype(F32)
    psels = [
        jnp.dot(jnp.concatenate([h * s for h in bhits], axis=1), turn, preferred_element_type=F32) for s in bsels
    ]

    def pick(sel, values):
        return jnp.dot(sel.astype(BF16), values, preferred_element_type=F32)

    def to_chunks(values, out):
        for b in range(blocks):
            wide[pl.ds(b, groups, stride=blocks), :] = values[:, b * LANES:(b + 1) * LANES]
        out[...] = wide[...].astype(BF16)

    def to_rows(ref):
        wide[...] = ref[...].astype(F32)
        return jnp.concatenate(
            [wide[pl.ds(b, groups, stride=blocks), :].astype(BF16) for b in range(blocks)], axis=1
        )

    span = (groups - 1) * blocks

    def exchange(src, dst, s):
        own = pl.ds(pl.multiple_of(e * blocks, blocks), blocks)

        def to(there):
            remote(
                src.at[pl.ds(pl.multiple_of(there * blocks, blocks), blocks)], dst.at[own],
                a2a_s.at[s], a2a_r.at[s], peer(there),
            ).start()

        ring = groups // 4
        for dz in (1, 0):
            z = (e // (2 * ring) + dz) % 2

            @pl.loop(0, ring - 1 + dz)
            def _(j):
                away = ring // 2 + (j + 1) // 2 * (1 - 2 * (j % 2))
                y = (e // 2 + away) % ring
                for dx in (1, 0):
                    to(z * (2 * ring) + y * 2 + (e + dx) % 2)

        to(e + 1 - 2 * (e % 2))
        dst[own, :] = src[own, :]
        whole = remote(src.at[pl.ds(0, span)], dst.at[pl.ds(0, span)], a2a_s.at[s], a2a_r.at[s], sib)
        sent.append(whole)
        return whole

    def ROWS(k):
        return pl.ds(pl.multiple_of(k * groups, groups), groups)

    came, shares, ons, sibs, passes, homes, pair_copies = {}, {}, {}, {}, {}, {}, {}

    def dispatch(u, sel, values):
        to_chunks(pick(sel, values), snd.at[u])
        came[u] = exchange(snd.at[u], rcv.at[u], u)

    def share_out(u):
        came[u].wait_recv()
        mine = rows.at[u, ROWS(q)]
        mine[...] = to_rows(rcv.at[u])
        shares[u] = (
            send(mine, mine, quad_s.at[u, 0], quad_r.at[u, 0], near),
            send(mine, mine, quad_s.at[u, 1], quad_r.at[u, 1], sib),
        )

    def hand_on(u):
        shares[u][0].wait_recv()
        other = rows.at[u, ROWS(near_q)]
        ons[u] = send(other, other, quad_s.at[u, 2], quad_r.at[u, 2], sib)

    def share_pairs(h):
        came[4 + h].wait_recv()
        pair_rows[h] = to_rows(rcv.at[4 + h])
        cols = [
            [pl.ds(pl.multiple_of((g * PARTS + (q + i) % PARTS) * part, part), part) for g in range(2)]
            for i in range(PARTS)
        ]
        pair_copies[h] = [
            send(
                pair_rows.at[h, :, cols[i][g]], pairs.at[h, ROWS(q), pl.ds(g * part, part)],
                pair_s.at[h, i - 1, g], pair_r.at[h, i - 1, g], (seg, e * PARTS + (q + i) % PARTS),
            )
            for i in range(1, PARTS)
            for g in range(2)
        ]
        for g in range(2):
            pairs[h, ROWS(q), g * part:(g + 1) * part] = pair_rows[h, :, cols[0][g]]

    def compute(u):
        shares[u][1].wait_recv()
        ons[u].wait_recv()
        if u < CAP:
            both = jnp.dot(rows[u], wgu_ref[...], preferred_element_type=F32)
            gate = both[:, :part]
            hidden = (gate / (1.0 + jnp.exp(-gate)) * both[:, part:]).astype(BF16)
            parts[u] = jnp.dot(hidden, wd_ref[...], preferred_element_type=F32).astype(BF16)
        else:
            h = u - CAP
            for one in pair_copies[h]:
                one.wait_recv()
            grad_hidden = lax.dot_general(
                rows[u], wd_ref[...], (((1,), (1,)), ((), ())), preferred_element_type=F32
            )
            a = pairs[h, :, :part].astype(F32)
            b = pairs[h, :, part:].astype(F32)
            sig = 1.0 / (1.0 + jnp.exp(-a))
            grad_gate = (grad_hidden * b * sig * (1.0 + a * (1.0 - sig))).astype(BF16)
            grad_upper = (grad_hidden * (a * sig)).astype(BF16)
            parts[u] = lax.dot_general(
                jnp.concatenate([grad_gate, grad_upper], axis=1), wgu_ref[...],
                (((1,), (1,)), ((), ())), preferred_element_type=F32,
            ).astype(BF16)
        sibs[u] = [
            send(parts.at[u, ROWS(x * 2 + 1 - c)], from_sib.at[u, x], red_s.at[u, x], red_r.at[u, x], sib)
            for x in range(2)
        ]

    def sum_core(u):
        for one in sibs[u]:
            one.wait_recv()
        passed[u] = (parts[u, ROWS(near_q), :].astype(F32) + from_sib[u, 1 - xl].astype(F32)).astype(BF16)
        passes[u] = send(passed.at[u], from_near.at[u], red_s.at[u, 2], red_r.at[u, 2], near)

    def go_home(u):
        passes[u].wait_recv()
        total = parts[u, ROWS(q), :].astype(F32) + from_sib[u, xl].astype(F32) + from_near[u].astype(F32)
        to_chunks(total, home_snd.at[u])
        homes[u] = exchange(home_snd.at[u], home_rcv.at[u], 6 + u)

    def combined(u, weight):
        homes[u].wait_recv()
        back = to_rows(home_rcv.at[u])
        high = weight.astype(BF16)
        low = (weight - high.astype(F32)).astype(BF16)
        return jnp.dot(high, back, preferred_element_type=F32) + jnp.dot(low, back, preferred_element_type=F32)

    def unstaged(i):
        shifts[i].wait_recv()
        v = landed[i].astype(F32)
        return jnp.concatenate([v[:tokens], v[tokens:]], axis=1)

    steps = 8
    step = width // steps

    def lay_out(first, last):
        @pl.loop(first, last)
        def _(i):
            some = pl.ds(pl.multiple_of(i * step, step), step)
            for g in range(2):
                wgu_ref[some, g * part:(g + 1) * part] = wgu_raw[some, g, :]

    arrived = unstaged(0)
    dispatch(0, fsels[0], arrived.astype(BF16))
    dispatch(1, fsels[1], arrived.astype(BF16))
    returning = unstaged(1)
    dispatch(2, bsels[0], returning.astype(BF16))
    dispatch(4, psels[0], saved_rows[...])
    for one in loads[7:]:
        one.wait()
    lay_out(0, steps)
    share_out(0)
    dispatch(3, bsels[1], returning.astype(BF16))
    share_out(1)
    dispatch(5, psels[1], saved_rows[...])
    share_out(2)
    hand_on(0)
    compute(0)
    hand_on(1)
    sum_core(0)
    share_pairs(0)
    compute(1)
    share_out(3)
    sum_core(1)
    hand_on(2)
    compute(2)
    go_home(0)
    share_pairs(1)
    sum_core(2)
    hand_on(3)
    go_home(1)
    compute(3)
    sum_core(3)
    go_home(2)
    mixed_f = combined(0, fweights[0])
    go_home(3)
    out[0] = (arrived + mixed_f + combined(1, fweights[1])).astype(BF16)
    mixed_b = combined(2, bweights[0])
    out[1] = (returning + mixed_b + combined(3, bweights[1])).astype(BF16)

    for one in sent:
        one.wait_send()


def on_device(
    groups, sections,
    forward_input, forward_routes, forward_gates, backward_grad, backward_routes, backward_gates,
    saved_gate_up, w_gate_up, w_down,
):
    _, tokens, width = forward_input.shape
    top = forward_routes.shape[-1]
    hidden = saved_gate_up.shape[-1]
    part = w_down.shape[1]
    hbm = pl.BlockSpec(memory_space=pl.ANY)
    long = groups * width // LANES
    row = jax.ShapeDtypeStruct((tokens, width), BF16)
    dma = pltpu.SemaphoreType.DMA
    units = 2 * CAP
    by_top = lambda v: jnp.transpose(v, (2, 0, 1))
    out = pl.pallas_call(
        functools.partial(on_chip, groups, sections),
        out_shape=jax.ShapeDtypeStruct((2, tokens, width), BF16),
        in_specs=[hbm] * 9,
        out_specs=pl.BlockSpec(memory_space=pltpu.VMEM),
        scratch_shapes=[
            pltpu.VMEM((tokens, width), BF16),
            pltpu.VMEM((tokens, width), BF16),
            pltpu.VMEM((top, 1, tokens), jnp.int32),
            pltpu.VMEM((top, 1, tokens), F32),
            pltpu.VMEM((top, 1, tokens), jnp.int32),
            pltpu.VMEM((top, 1, tokens), F32),
            pltpu.VMEM((tokens * top, 2, hidden), BF16),
            pltpu.VMEM((width, 2, part), BF16),
            pltpu.VMEM((part, width), BF16),
            pltpu.VMEM((2, 2 * tokens, width // 2), BF16),
            pltpu.VMEM((2, 2 * tokens, width // 2), BF16),
            pltpu.VMEM((width, 2 * part), BF16),
            pltpu.VMEM((tokens * top, 2 * hidden), BF16),
            pltpu.VMEM((long, LANES), F32),
            pltpu.VMEM((units + CAP, long, LANES), BF16),
            pltpu.VMEM((units + CAP, long, LANES), BF16),
            pltpu.VMEM((units, PARTS * groups, width), BF16),
            pltpu.VMEM((CAP, groups, 2 * hidden), BF16),
            pltpu.VMEM((CAP, PARTS * groups, 2 * part), BF16),
            pltpu.VMEM((units, PARTS * groups, width), BF16),
            pltpu.VMEM((units, 2, groups, width), BF16),
            pltpu.VMEM((units, groups, width), BF16),
            pltpu.VMEM((units, groups, width), BF16),
            pltpu.VMEM((units, long, LANES), BF16),
            pltpu.VMEM((units, long, LANES), BF16),
            dma((9,)), dma((2,)), dma((2,)),
            dma((2 * units + CAP,)), dma((2 * units + CAP,)), dma((units, 3)), dma((units, 3)),
            dma((CAP, PARTS - 1, 2)), dma((CAP, PARTS - 1, 2)), dma((units, 3)), dma((units, 3)),
        ],
        compiler_params=pltpu.CompilerParams(
            collective_id=0, has_side_effects=True, vmem_limit_bytes=62 * 2**20
        ),
    )(
        forward_input[0], backward_grad[0], by_top(forward_routes), by_top(forward_gates),
        by_top(backward_routes), by_top(backward_gates),
        saved_gate_up[0].reshape(tokens * top, 2, hidden), w_gate_up[0], w_down[0],
    )
    return out[:1], out[1:]


def solution(mesh):
    spec = P("segment", "expert", None)
    placed = (
        spec, spec, spec, spec, spec, spec,
        P("segment", "expert", None, None, None),
        P("segment", None, None, "expert"),
        spec,
    )
    return jax.shard_map(
        functools.partial(on_device, mesh.shape["expert"] // PARTS, mesh.shape["segment"]),
        mesh=mesh,
        in_specs=placed,
        out_specs=(spec, spec),
        check_vma=False,
    )
```

```python
import functools

import jax
import jax.numpy as jnp
from jax import lax
from jax.experimental import pallas as pl
from jax.experimental.pallas import tpu as pltpu
from jax.sharding import PartitionSpec as P

CAP = 2
PARTS = 4
LANES = 128
MESH = pl.DeviceIdType.MESH
F32 = jnp.float32
BF16 = jnp.bfloat16


def on_chip(
    groups, sections,
    fwd_hbm, bwd_hbm, froute_hbm, fgate_hbm, broute_hbm, bgate_hbm, saved_hbm, wgu_hbm, wd_hbm,
    out,
    fwd_ref, bwd_ref, froute_ref, fgate_ref, broute_ref, bgate_ref, saved_ref, wgu_raw, wd_ref,
    stage, landed, wgu_ref, saved_rows, wide,
    snd, rcv, rows, pair_rows, pairs, parts, from_sib, passed, from_near, home_snd, home_rcv,
    load_s, shift_s, shift_r, a2a_s, a2a_r, quad_s, quad_r, pair_s, pair_r, red_s, red_r,
):
    seg = lax.axis_index("segment")
    idx = lax.axis_index("expert")
    e = idx // PARTS
    q = idx % PARTS
    xl = q // 2
    c = q % 2
    near_q = (1 - xl) * 2 + c
    sib = (seg, e * PARTS + xl * 2 + (1 - c))
    near = (seg, e * PARTS + near_q)
    width = wd_ref.shape[1]
    part = wd_ref.shape[0]
    top, _, tokens = froute_ref.shape
    blocks = width // LANES
    half = width // 2
    sent = []

    def remote(src, dst, ss, rs, where):
        return pltpu.make_async_remote_copy(
            src_ref=src, dst_ref=dst, send_sem=ss, recv_sem=rs, device_id=where, device_id_type=MESH
        )

    def send(*what):
        copy = remote(*what)
        copy.start()
        sent.append(copy)
        return copy

    def peer(there):
        return (seg, there * PARTS + (q + 2 * ((e + there) % 2)) % PARTS)

    loads = [
        pltpu.make_async_copy(there, here, load_s.at[i])
        for i, (there, here) in enumerate((
            (fwd_hbm, fwd_ref), (bwd_hbm, bwd_ref), (froute_hbm, froute_ref), (fgate_hbm, fgate_ref),
            (broute_hbm, broute_ref), (bgate_hbm, bgate_ref), (saved_hbm, saved_ref), (wgu_hbm, wgu_raw),
            (wd_hbm, wd_ref),
        ))
    ]
    for one in loads:
        one.start()

    barrier = pltpu.get_barrier_semaphore()

    @pl.loop(1, groups)
    def _(i):
        pl.semaphore_signal(barrier, inc=1, device_id=peer((e + i) % groups), device_id_type=MESH)

    for i in range(1, PARTS):
        pl.semaphore_signal(barrier, inc=1, device_id=(seg, e * PARTS + (q + i) % PARTS), device_id_type=MESH)
    after = (seg + 1) % sections
    before = (seg + sections - 1) % sections
    for there in (after, before):
        pl.semaphore_signal(barrier, inc=1, device_id=(there, idx), device_id_type=MESH)

    for i, ref in enumerate((fwd_ref, bwd_ref)):
        loads[i].wait()
        v = ref[...].astype(F32)
        stage[i] = jnp.concatenate([v[:, :half], v[:, half:]], axis=0).astype(BF16)

    pl.semaphore_wait(barrier, groups + PARTS)
    shifts = [
        send(stage.at[i], landed.at[i], shift_s.at[i], shift_r.at[i], (there, idx))
        for i, there in enumerate((after, before))
    ]

    for one in loads[2:7]:
        one.wait()
    for g in range(2):
        saved_rows[:, g * half:(g + 1) * half] = saved_ref[:, g, :]

    row_e = lax.broadcasted_iota(jnp.int32, (groups, tokens), 0)
    prior = (
        lax.broadcasted_iota(jnp.int32, (tokens, tokens), 0) < lax.broadcasted_iota(jnp.int32, (tokens, tokens), 1)
    ).astype(F32)

    def matches(route_ref, gate_ref):
        hits = [(row_e == route_ref[k]).astype(F32) for k in range(top)]
        named = functools.reduce(jnp.add, hits)
        rank = jnp.dot(named, prior, preferred_element_type=F32)
        gate = functools.reduce(jnp.add, [hits[k] * gate_ref[k] for k in range(top)])
        sels = [jnp.where(rank == float(h), named, 0.0) for h in range(CAP)]
        return hits, sels, [(gate * s).T for s in sels]

    bhits, bsels, bweights = matches(broute_ref, bgate_ref)
    fhits, fsels, fweights = matches(froute_ref, fgate_ref)
    n = top * tokens
    kt = lax.broadcasted_iota(jnp.int32, (n, n), 0)
    tk = lax.broadcasted_iota(jnp.int32, (n, n), 1)
    turn = ((kt % tokens) * top + kt // tokens == tk).astype(F32)
    psels = [
        jnp.dot(jnp.concatenate([h * s for h in bhits], axis=1), turn, preferred_element_type=F32) for s in bsels
    ]

    def pick(sel, values):
        return jnp.dot(sel.astype(BF16), values, preferred_element_type=F32)

    def to_chunks(values, out):
        for b in range(blocks):
            wide[pl.ds(b, groups, stride=blocks), :] = values[:, b * LANES:(b + 1) * LANES]
        out[...] = wide[...].astype(BF16)

    def to_rows(ref):
        wide[...] = ref[...].astype(F32)
        return jnp.concatenate(
            [wide[pl.ds(b, groups, stride=blocks), :].astype(BF16) for b in range(blocks)], axis=1
        )

    span = (groups - 1) * blocks

    def exchange(src, dst, s):
        own = pl.ds(pl.multiple_of(e * blocks, blocks), blocks)

        def to(there):
            remote(
                src.at[pl.ds(pl.multiple_of(there * blocks, blocks), blocks)], dst.at[own],
                a2a_s.at[s], a2a_r.at[s], peer(there),
            ).start()

        ring = groups // 4
        for dz in (1, 0):
            z = (e // (2 * ring) + dz) % 2

            @pl.loop(0, ring - 1 + dz)
            def _(j):
                away = ring // 2 + (j + 1) // 2 * (1 - 2 * (j % 2))
                y = (e // 2 + away) % ring
                for dx in (1, 0):
                    to(z * (2 * ring) + y * 2 + (e + dx) % 2)

        to(e + 1 - 2 * (e % 2))
        dst[own, :] = src[own, :]
        whole = remote(src.at[pl.ds(0, span)], dst.at[pl.ds(0, span)], a2a_s.at[s], a2a_r.at[s], sib)
        sent.append(whole)
        return whole

    def ROWS(k):
        return pl.ds(pl.multiple_of(k * groups, groups), groups)

    came, shares, ons, sibs, passes, homes, pair_copies = {}, {}, {}, {}, {}, {}, {}

    def dispatch(u, sel, values):
        to_chunks(pick(sel, values), snd.at[u])
        came[u] = exchange(snd.at[u], rcv.at[u], u)

    def share_out(u):
        came[u].wait_recv()
        mine = rows.at[u, ROWS(q)]
        mine[...] = to_rows(rcv.at[u])
        shares[u] = (
            send(mine, mine, quad_s.at[u, 0], quad_r.at[u, 0], near),
            send(mine, mine, quad_s.at[u, 1], quad_r.at[u, 1], sib),
        )

    def hand_on(u):
        shares[u][0].wait_recv()
        other = rows.at[u, ROWS(near_q)]
        ons[u] = send(other, other, quad_s.at[u, 2], quad_r.at[u, 2], sib)

    def share_pairs(h):
        came[4 + h].wait_recv()
        pair_rows[h] = to_rows(rcv.at[4 + h])
        cols = [
            [pl.ds(pl.multiple_of((g * PARTS + (q + i) % PARTS) * part, part), part) for g in range(2)]
            for i in range(PARTS)
        ]
        pair_copies[h] = [
            send(
                pair_rows.at[h, :, cols[i][g]], pairs.at[h, ROWS(q), pl.ds(g * part, part)],
                pair_s.at[h, i - 1, g], pair_r.at[h, i - 1, g], (seg, e * PARTS + (q + i) % PARTS),
            )
            for i in range(1, PARTS)
            for g in range(2)
        ]
        for g in range(2):
            pairs[h, ROWS(q), g * part:(g + 1) * part] = pair_rows[h, :, cols[0][g]]

    def compute(u):
        shares[u][1].wait_recv()
        ons[u].wait_recv()
        if u < CAP:
            both = jnp.dot(rows[u], wgu_ref[...], preferred_element_type=F32)
            gate = both[:, :part]
            hidden = (gate / (1.0 + jnp.exp(-gate)) * both[:, part:]).astype(BF16)
            parts[u] = jnp.dot(hidden, wd_ref[...], preferred_element_type=F32).astype(BF16)
        else:
            h = u - CAP
            for one in pair_copies[h]:
                one.wait_recv()
            grad_hidden = lax.dot_general(
                rows[u], wd_ref[...], (((1,), (1,)), ((), ())), preferred_element_type=F32
            )
            a = pairs[h, :, :part].astype(F32)
            b = pairs[h, :, part:].astype(F32)
            sig = 1.0 / (1.0 + jnp.exp(-a))
            grad_gate = (grad_hidden * b * sig * (1.0 + a * (1.0 - sig))).astype(BF16)
            grad_upper = (grad_hidden * (a * sig)).astype(BF16)
            parts[u] = lax.dot_general(
                jnp.concatenate([grad_gate, grad_upper], axis=1), wgu_ref[...],
                (((1,), (1,)), ((), ())), preferred_element_type=F32,
            ).astype(BF16)
        sibs[u] = [
            send(parts.at[u, ROWS(x * 2 + 1 - c)], from_sib.at[u, x], red_s.at[u, x], red_r.at[u, x], sib)
            for x in range(2)
        ]

    def sum_core(u):
        for one in sibs[u]:
            one.wait_recv()
        passed[u] = (parts[u, ROWS(near_q), :].astype(F32) + from_sib[u, 1 - xl].astype(F32)).astype(BF16)
        passes[u] = send(passed.at[u], from_near.at[u], red_s.at[u, 2], red_r.at[u, 2], near)

    def go_home(u):
        passes[u].wait_recv()
        total = parts[u, ROWS(q), :].astype(F32) + from_sib[u, xl].astype(F32) + from_near[u].astype(F32)
        to_chunks(total, home_snd.at[u])
        homes[u] = exchange(home_snd.at[u], home_rcv.at[u], 6 + u)

    def combined(u, weight):
        homes[u].wait_recv()
        back = to_rows(home_rcv.at[u])
        high = weight.astype(BF16)
        low = (weight - high.astype(F32)).astype(BF16)
        return jnp.dot(high, back, preferred_element_type=F32) + jnp.dot(low, back, preferred_element_type=F32)

    def unstaged(i):
        shifts[i].wait_recv()
        v = landed[i].astype(F32)
        return jnp.concatenate([v[:tokens], v[tokens:]], axis=1)

    steps = 8
    step = width // steps

    def lay_out(first, last):
        @pl.loop(first, last)
        def _(i):
            some = pl.ds(pl.multiple_of(i * step, step), step)
            for g in range(2):
                wgu_ref[some, g * part:(g + 1) * part] = wgu_raw[some, g, :]

    arrived = unstaged(0)
    dispatch(0, fsels[0], arrived.astype(BF16))
    dispatch(1, fsels[1], arrived.astype(BF16))
    returning = unstaged(1)
    dispatch(2, bsels[0], returning.astype(BF16))
    dispatch(4, psels[0], saved_rows[...])
    for one in loads[7:]:
        one.wait()
    lay_out(0, steps)
    share_out(0)
    dispatch(3, bsels[1], returning.astype(BF16))
    share_out(1)
    dispatch(5, psels[1], saved_rows[...])
    share_out(2)
    hand_on(0)
    compute(0)
    hand_on(1)
    sum_core(0)
    share_pairs(0)
    compute(1)
    share_out(3)
    sum_core(1)
    hand_on(2)
    compute(2)
    go_home(0)
    sum_core(2)
    share_pairs(1)
    hand_on(3)
    go_home(1)
    compute(3)
    sum_core(3)
    go_home(2)
    mixed_f = combined(0, fweights[0])
    go_home(3)
    out[0] = (arrived + mixed_f + combined(1, fweights[1])).astype(BF16)
    mixed_b = combined(2, bweights[0])
    out[1] = (returning + mixed_b + combined(3, bweights[1])).astype(BF16)

    for one in sent:
        one.wait_send()


def on_device(
    groups, sections,
    forward_input, forward_routes, forward_gates, backward_grad, backward_routes, backward_gates,
    saved_gate_up, w_gate_up, w_down,
):
    _, tokens, width = forward_input.shape
    top = forward_routes.shape[-1]
    hidden = saved_gate_up.shape[-1]
    part = w_down.shape[1]
    hbm = pl.BlockSpec(memory_space=pl.ANY)
    long = groups * width // LANES
    row = jax.ShapeDtypeStruct((tokens, width), BF16)
    dma = pltpu.SemaphoreType.DMA
    units = 2 * CAP
    by_top = lambda v: jnp.transpose(v, (2, 0, 1))
    out = pl.pallas_call(
        functools.partial(on_chip, groups, sections),
        out_shape=jax.ShapeDtypeStruct((2, tokens, width), BF16),
        in_specs=[hbm] * 9,
        out_specs=pl.BlockSpec(memory_space=pltpu.VMEM),
        scratch_shapes=[
            pltpu.VMEM((tokens, width), BF16),
            pltpu.VMEM((tokens, width), BF16),
            pltpu.VMEM((top, 1, tokens), jnp.int32),
            pltpu.VMEM((top, 1, tokens), F32),
            pltpu.VMEM((top, 1, tokens), jnp.int32),
            pltpu.VMEM((top, 1, tokens), F32),
            pltpu.VMEM((tokens * top, 2, hidden), BF16),
            pltpu.VMEM((width, 2, part), BF16),
            pltpu.VMEM((part, width), BF16),
            pltpu.VMEM((2, 2 * tokens, width // 2), BF16),
            pltpu.VMEM((2, 2 * tokens, width // 2), BF16),
            pltpu.VMEM((width, 2 * part), BF16),
            pltpu.VMEM((tokens * top, 2 * hidden), BF16),
            pltpu.VMEM((long, LANES), F32),
            pltpu.VMEM((units + CAP, long, LANES), BF16),
            pltpu.VMEM((units + CAP, long, LANES), BF16),
            pltpu.VMEM((units, PARTS * groups, width), BF16),
            pltpu.VMEM((CAP, groups, 2 * hidden), BF16),
            pltpu.VMEM((CAP, PARTS * groups, 2 * part), BF16),
            pltpu.VMEM((units, PARTS * groups, width), BF16),
            pltpu.VMEM((units, 2, groups, width), BF16),
            pltpu.VMEM((units, groups, width), BF16),
            pltpu.VMEM((units, groups, width), BF16),
            pltpu.VMEM((units, long, LANES), BF16),
            pltpu.VMEM((units, long, LANES), BF16),
            dma((9,)), dma((2,)), dma((2,)),
            dma((2 * units + CAP,)), dma((2 * units + CAP,)), dma((units, 3)), dma((units, 3)),
            dma((CAP, PARTS - 1, 2)), dma((CAP, PARTS - 1, 2)), dma((units, 3)), dma((units, 3)),
        ],
        compiler_params=pltpu.CompilerParams(
            collective_id=0, has_side_effects=True, vmem_limit_bytes=62 * 2**20
        ),
    )(
        forward_input[0], backward_grad[0], by_top(forward_routes), by_top(forward_gates),
        by_top(backward_routes), by_top(backward_gates),
        saved_gate_up[0].reshape(tokens * top, 2, hidden), w_gate_up[0], w_down[0],
    )
    return out[:1], out[1:]


def solution(mesh):
    spec = P("segment", "expert", None)
    placed = (
        spec, spec, spec, spec, spec, spec,
        P("segment", "expert", None, None, None),
        P("segment", None, None, "expert"),
        spec,
    )
    return jax.shard_map(
        functools.partial(on_device, mesh.shape["expert"] // PARTS, mesh.shape["segment"]),
        mesh=mesh,
        in_specs=placed,
        out_specs=(spec, spec),
        check_vma=False,
    )
```
